128 devices in a mesh: box: 32 (over z, x, core), inc: 4 (over y).
Axes of the slice: x: 4, y: 4, z: 4, core: 2. Of those that a mesh axis runs over, the one named last changes fastest.
Arguments:
- leaves: float32 [1024, 2, 16, 2048], P('box', None, 'inc'), parts along dimension 2, may hold values from -6 to 6
- theta_a: float32 [32, 64], replicated, may hold values from -1 to 1
- phi_a: float32 [64, 128], replicated, may hold values from -0.75 to 0.75
- shift_b: float32 [8, 64, 128], replicated, may hold values from -3.140625 to 3.140625
- theta_b: float32 [64, 128], replicated, may hold values from -0.75 to 0.75
- phi_b: float32 [128, 256], replicated, may hold values from -0.5 to 0.5
- shift_c: float32 [8, 128, 256], replicated, may hold values from -3.140625 to 3.140625
- parent_map: int32 [128], replicated, may hold values from 0 to 15
- inter_list: int32 [128, 32], replicated, may hold values from 0 to 127
- op_index: int32 [128, 32], replicated, may hold values from 0 to 315
- trans_ops: float32 [2, 316, 64, 128], P(None, None, 'box'), may hold values from -0.75 to 0.75
Outputs:
- parents: float32 [16, 2, 16, 128, 256], P(None, None, 'inc', 'box'), parts along dimension 2
- incoming: float32 [128, 2, 16, 64, 128], P('box', None, 'inc'), parts along dimension 2
The draws below stay inside these ranges and needn't reach their ends.
There are 4 independent parts, one for each index of `inc`. The reference program is written for one: setup_inputs(seed, part) draws one part's arguments, and reference() takes and returns one part's arrays. A program takes and returns all parts, laid end to end along the dimension named above; an argument that names none is the same for every part. Nothing has to cross between parts.
All inputs are finite; a program needn't handle non-finite values.
Results may differ from the reference program's by a relative error of at most 0.00007.
Values sent between devices are 32-bit elements; how exact they have to be, the bound alone decides.
A program may use at most 128 MiB of HBM per device.

```python
import jax
import jax.numpy as jnp
from jax import lax

TA = 32
PA = 64
TB = 64
PB = 128
TC = 128
PC = 256
NI = 4
LIST = 32
NOPS = 316
NA = 1024
NB = 128
NC = 16


def with_ends(drawn, key, low, top_value):
    shape = drawn.shape
    index_at = [jax.random.randint(jax.random.fold_in(key, axis), (), 0, shape[axis]) for axis in range(len(shape))]
    drawn = drawn.at[tuple(index_at)].set(low)
    longest = shape.index(max(shape))
    index_at[longest] = (index_at[longest] + 1) % shape[longest]
    return drawn.at[tuple(index_at)].set(top_value)


def block_scale(rng, extent, pieces, smallest, largest):
    factor_of = 1.0
    for axis_at, shards_of in pieces:
        draws = jax.random.uniform(jax.random.fold_in(jax.random.fold_in(rng, 6), axis_at), (shards_of,), jnp.float32, smallest / len(pieces), largest / len(pieces))
        factor_of = factor_of * jnp.repeat(jnp.exp(draws), extent[axis_at] // shards_of).reshape((-1,) + (1,) * (len(extent) - 1 - axis_at))
    return factor_of


def gaussian(key, shape, deviation, reach, cuts=(), kind=jnp.bfloat16):
    level = block_scale(key, shape, cuts, -0.22, 0.18) if cuts else 1.0
    entries = jax.random.normal(key, shape, jnp.float32) * deviation * level
    return jnp.minimum(jnp.maximum(entries, -reach), reach).astype(kind)


def setup_inputs(seed: int = 0, part: int = 0) -> dict:
    keys = jax.random.split(jax.random.key(seed), 12)
    own_keys = jax.random.split(jax.random.fold_in(keys[11], part), 12)
    return {
        "leaves": gaussian(own_keys[0], (NA, 2, NI, TA * PA), 1.0, 6.0, ((0, 32),), jnp.float32),
        "theta_a": gaussian(keys[1], (TA, TB), TA ** -0.5, 1.0, (), jnp.float32),
        "phi_a": gaussian(keys[2], (PA, PB), PA ** -0.5, 0.75, (), jnp.float32),
        "shift_b": jnp.clip(jax.random.uniform(keys[3], (8, TB, PB), jnp.float32, -3.140625, 3.140625), -3.140625, 3.140625),
        "theta_b": gaussian(keys[4], (TB, TC), TB ** -0.5, 0.75, (), jnp.float32),
        "phi_b": gaussian(keys[5], (PB, PC), PB ** -0.5, 0.5, (), jnp.float32),
        "shift_c": jnp.clip(jax.random.uniform(keys[6], (8, TC, PC), jnp.float32, -3.140625, 3.140625), -3.140625, 3.140625),
        "parent_map": with_ends(jax.random.randint(keys[7], (NB,), 0, NC), jax.random.fold_in(keys[7], 1), 0, NC - 1).astype(jnp.int32),
        "inter_list": with_ends(jax.random.randint(keys[8], (NB, LIST), 0, NB), jax.random.fold_in(keys[8], 1), 0, NB - 1).astype(jnp.int32),
        "op_index": with_ends(jax.random.randint(keys[9], (NB, LIST), 0, NOPS), jax.random.fold_in(keys[9], 1), 0, NOPS - 1).astype(jnp.int32),
        "trans_ops": gaussian(keys[10], (2, NOPS, TB, PB), (2 * LIST) ** -0.5, 0.75, ((2, 32),), jnp.float32),
    }


merge_weight = 0.35


def upsample(field, polar, azimuth):
    step_one = jnp.einsum('bcitp,tu->bciup', field, polar, precision=lax.Precision.HIGHEST)
    return jnp.einsum('bciup,pv->bciuv', step_one, azimuth, precision=lax.Precision.HIGHEST)


def rotate(field, angle):
    cosine = jnp.cos(angle)[:, None]
    sine = jnp.sin(angle)[:, None]
    real_part = field[:, 0]
    imag_part = field[:, 1]
    return jnp.stack([cosine * real_part - sine * imag_part, sine * real_part + cosine * imag_part], axis=1)


def reference(leaves, theta_a, phi_a, shift_b, theta_b, phi_b, shift_c, parent_map, inter_list, op_index, trans_ops):
    count_a = leaves.shape[0]
    incid = leaves.shape[2]
    count_b = count_a // 8
    count_c = count_b // 8
    leaf_grid = leaves.reshape(count_a, 2, incid, TA, PA)
    leaf_up = upsample(leaf_grid, theta_a, phi_a)
    turned = rotate(leaf_up, jnp.tile(shift_b, (count_b, 1, 1)))
    middle = merge_weight * jnp.sum(turned.reshape(count_b, 8, 2, incid, TB, PB), axis=1)
    middle_up = upsample(middle, theta_b, phi_b)
    shifted = rotate(middle_up, jnp.tile(shift_c, (count_c, 1, 1)))
    owners = (parent_map[None, :] == jnp.arange(count_c, dtype=jnp.int32)[:, None]).astype(jnp.float32)
    parents = merge_weight * jnp.einsum('pb,bciuv->pciuv', owners, shifted, precision=lax.Precision.HIGHEST)

    def one_target(pair):
        sources, operators = pair
        picked = middle[sources]
        table = trans_ops[:, operators]
        real_part = jnp.sum(table[0][:, None] * picked[:, 0] - table[1][:, None] * picked[:, 1], axis=0)
        imag_part = jnp.sum(table[0][:, None] * picked[:, 1] + table[1][:, None] * picked[:, 0], axis=0)
        return jnp.stack([real_part, imag_part], axis=0)

    incoming = lax.map(one_target, (inter_list, op_index))
    return parents, incoming
```

```python
import functools

import jax
import jax.numpy as jnp
from jax import lax
from jax.experimental import pallas as pl
from jax.experimental.pallas import tpu as pltpu
from jax.sharding import PartitionSpec as P

F32 = jnp.float32
BF16 = jnp.bfloat16
MESH = pl.DeviceIdType.MESH
N = 32
NOPS = 316
LIST = 32
MERGE = 0.35

HOPS = (
    (2, 2),
    (2, 1), (2, 3), (1, 2), (3, 2),
    (0, 2), (2, 0),
    (1, 3), (3, 1),
    (1, 1), (3, 3),
    (0, 1), (0, 3), (1, 0), (3, 0),
)


def dot(a, b):
    return lax.dot_general(a, b, (((1,), (0,)), ((), ())), preferred_element_type=F32)


def dot_t(a, b):
    return lax.dot_general(a, b, (((0,), (0,)), ((), ())), preferred_element_type=F32)


def split(x):
    hi = x.astype(BF16)
    lo = (x - hi.astype(F32)).astype(BF16)
    return hi, lo


def split3(x):
    hi = x.astype(BF16)
    rest = x - hi.astype(F32)
    mid = rest.astype(BF16)
    lo = (rest - mid.astype(F32)).astype(BF16)
    return hi, mid, lo


def cos_sin(angle):
    h = angle * 0.5
    g = h * h
    s = 1.0 / 6227020800.0
    for c in (-1.0 / 39916800.0, 1.0 / 362880.0, -1.0 / 5040.0, 1.0 / 120.0, -1.0 / 6.0, 1.0):
        s = s * g + c
    s = s * h
    c0 = 1.0 / 479001600.0
    for c in (-1.0 / 3628800.0, 1.0 / 40320.0, -1.0 / 720.0, 1.0 / 24.0, -0.5, 1.0):
        c0 = c0 * g + c
    return 1.0 - 2.0 * s * s, 2.0 * s * c0


def iota(shape, dim):
    return lax.broadcasted_iota(jnp.int32, shape, dim)


def onehot(cond):
    return jnp.where(cond, 1.0, 0.0).astype(F32).astype(BF16)


def kernel(
    leaves_hbm, theta_a_hbm, phi_a_hbm, shift_b_hbm, theta_b_hbm, phi_b_hbm, shift_c_hbm,
    pmap_hbm, list_hbm, ops_hbm, trans_hbm,
    parents_ref, incoming_ref,
    leaves, theta_a, phi_a, shift_b, theta_b, phi_b, shift_c, pmap, ilist, iops, trans,
    q3, w3, v3, tab, acc, gains, cs,
    buf_a, recv_a, buf_b, recv_b, buf_c, recv_c, azi, group, total,
    in_sem, leaf_sem, send_a, got_a, send_b, got_b, send_c, got_c,
):
    me = lax.axis_index("box")
    z, x, core = me // 8, (me // 2) % 4, me % 2
    zs = [((z + k) % 4) * 8 for k in range(4)]
    xs = [((x + k) % 4) * 2 for k in range(4)]
    cores = [core, 1 - core]
    partners = [zs[dz] + xs[dx] + cores[dc] for dz, dx in HOPS for dc in range(2)]
    partners.append(zs[0] + xs[0] + cores[1])

    barrier = pltpu.get_barrier_semaphore()
    for d in partners:
        pl.semaphore_signal(barrier, inc=1, device_id={"box": d}, device_id_type=MESH)

    def fetch(k, src, dst):
        copy = pltpu.make_async_copy(src, dst, in_sem.at[k])
        copy.start()
        return copy

    get_theta_a = fetch(0, theta_a_hbm, theta_a)
    get_phi_a = fetch(1, phi_a_hbm, phi_a)
    get_leaves = []
    for q in range(4):
        copy = pltpu.make_async_copy(
            leaves_hbm.at[pl.ds(8 * q, 8)], leaves.at[pl.ds(8 * q, 8)], leaf_sem.at[q]
        )
        copy.start()
        get_leaves.append(copy)
    get_shift_b = fetch(2, shift_b_hbm, shift_b)
    get_theta_b = fetch(3, theta_b_hbm, theta_b)
    get_trans = fetch(4, trans_hbm, trans)
    get_list = fetch(5, list_hbm, ilist)
    get_ops = fetch(6, ops_hbm, iops)
    get_phi_b = fetch(7, phi_b_hbm, phi_b)
    get_pmap = fetch(8, pmap_hbm, pmap)
    get_shift_c = fetch(
        9, shift_c_hbm.at[:, pl.ds(pl.multiple_of(8 * (me // 2), 8), 8), :], shift_c
    )

    get_phi_a.wait()
    for i, half in enumerate(split(phi_a[...])):
        none = jnp.zeros_like(half)
        both = jnp.concatenate(
            [jnp.concatenate([half, none], 1), jnp.concatenate([none, half], 1)], 0
        )
        if i == 0:
            q3[0:128, :] = both
            q3[128:256, :] = both
        else:
            q3[256:384, :] = both

    get_theta_a.wait()
    col = iota((32, 128), 1)
    pick_t = onehot(iota((32, 128), 0) == 2 * ((col % 64) // 4) + col // 64)
    rep_u = onehot(iota((256, 64), 1) == iota((256, 64), 0) // 4)
    same = iota((256, 128), 0) % 4 == iota((256, 128), 1) % 4
    for i, half in enumerate(split(theta_a[...])):
        wide = dot(rep_u, dot_t(half, pick_t).astype(BF16))
        wide = jnp.where(same, wide, 0.0).astype(BF16)
        if i == 0:
            w3[:, 0:128] = wide
            w3[:, 256:384] = wide
        else:
            w3[:, 128:256] = wide

    get_shift_b.wait()
    rep_u3 = jnp.concatenate([rep_u, rep_u, rep_u], 1)

    @pl.loop(0, 8)
    def _(o):
        cosine, sine = cos_sin(shift_b[o])
        pair = MERGE * jnp.concatenate([cosine, sine], 1)
        tab[o] = dot(rep_u3, jnp.concatenate(split3(pair), 0))

    get_theta_b.wait()
    pick_u = onehot(iota((64, 256), 0) == iota((64, 256), 1) // 4)
    row = iota((512, 128), 0)
    rep_u2 = onehot(iota((512, 128), 1) == 4 * (row // 16) + row % 4)
    same = (iota((512, 256), 0) % 16) // 4 == iota((512, 256), 1) % 4
    for i, half in enumerate(split(theta_b[...])):
        wide = dot(rep_u2, dot_t(half, pick_u).astype(BF16))
        wide = jnp.where(same, wide, 0.0).astype(BF16)
        if i == 0:
            v3[:, 0:256] = wide
            v3[:, 512:768] = wide
        else:
            v3[:, 256:512] = wide

    def compute(q):
        def one_leaf(o, carry):
            pattern = leaves[8 * q + o].reshape(128, 128)
            hi, lo = split(pattern)
            y = dot(jnp.concatenate([hi, lo, hi], 1), q3[...])
            y = jnp.concatenate(
                [
                    jnp.concatenate([y[0:64, 0:128], y[64:128, 0:128]], 1),
                    jnp.concatenate([y[0:64, 128:256], y[64:128, 128:256]], 1),
                ],
                0,
            )
            hi, lo = split(y)
            up = dot(w3[...], jnp.concatenate([hi, hi, lo], 0))
            cosine, sine = tab[o, :, 0:128], tab[o, :, 128:256]
            re, im = up[:, 0:128], up[:, 128:256]
            turned = jnp.concatenate([cosine * re - sine * im, sine * re + cosine * im], 1)
            acc[...] += turned
            return carry

        acc[...] = jnp.zeros_like(acc)
        lax.fori_loop(0, 8, one_leaf, 0)
        middle = acc[...]
        for c in range(2):
            buf_a[q, :, c] = middle[:, 128 * c : 128 * c + 128].reshape(32, 8, 128)
        hi, lo = split(middle)
        polar = dot(v3[...], jnp.concatenate([hi, hi, lo], 0))
        for c in range(2):
            buf_b[q, :, c] = polar[:, 128 * c : 128 * c + 128].reshape(32, 16, 128)
        recv_a[4 * me + q] = buf_a[q, me]
        recv_b[4 * me + q] = buf_b[q, me]

    def send(q):
        for buf, recv, send_sem, got_sem in (
            (buf_a, recv_a, send_a, got_a),
            (buf_b, recv_b, send_b, got_b),
        ):
            for d in partners:
                pltpu.make_async_remote_copy(
                    src_ref=buf.at[q, d],
                    dst_ref=recv.at[4 * me + q],
                    send_sem=send_sem,
                    recv_sem=got_sem,
                    device_id={"box": d},
                    device_id_type=MESH,
                ).start()

    get_leaves[0].wait()
    compute(0)
    pl.semaphore_wait(barrier, N - 1)
    send(0)
    for q in range(1, 4):
        get_leaves[q].wait()

    @pl.loop(1, 4)
    def _(q):
        compute(q)
        send(q)

    get_trans.wait()
    upper = iota((8, 128), 0) < 4

    @pl.loop(0, NOPS // 4)
    def _(k):
        for j in range(4):
            for c in range(2):
                two = trans[c, 4 * k + j]
                gains[4 * k + j, c] = jnp.where(
                    upper,
                    jnp.broadcast_to(two[0:1], (8, 128)),
                    jnp.broadcast_to(two[1:2], (8, 128)),
                )

    def every(ref, send_sem, got_sem):
        return pltpu.make_async_remote_copy(
            src_ref=ref,
            dst_ref=ref,
            send_sem=send_sem,
            recv_sem=got_sem,
            device_id={"box": partners[-1]},
            device_id_type=MESH,
        )

    all_a = every(recv_a.at[pl.ds(0, 124)], send_a, got_a)
    all_b = every(recv_b.at[pl.ds(0, 124)], send_b, got_b)
    all_c = every(recv_c.at[:, :, pl.ds(0, 248), :], send_c, got_c)
    get_list.wait()
    get_ops.wait()
    all_a.wait_recv()

    def translate(d, put):
        @pl.loop(0, 4)
        def _(k):
            t = 4 * d + k
            sums = [jnp.zeros((8, 128), F32) for _ in range(4)]
            for j in range(LIST):
                s, o = ilist[j, t], iops[j, t]
                sr, si = recv_a[s, 0], recv_a[s, 1]
                gr, gi = gains[o, 0], gains[o, 1]
                sums[0] += gr * sr
                sums[1] += gi * si
                sums[2] += gr * si
                sums[3] += gi * sr
            put(k, sums[0] - sums[1], sums[2] + sums[3])

    for d in partners:

        def put(k, re, im, d=d):
            buf_c[d, k, 0] = re
            buf_c[d, k, 1] = im

        translate(d, put)
        pltpu.make_async_remote_copy(
            src_ref=buf_c.at[d],
            dst_ref=recv_c.at[:, :, pl.ds(pl.multiple_of(8 * me, 8), 8), :],
            send_sem=send_c,
            recv_sem=got_c,
            device_id={"box": d},
            device_id_type=MESH,
        ).start()

    def put_own(k, re, im):
        recv_c[k, 0, pl.ds(pl.multiple_of(8 * me, 8), 8), :] = re
        recv_c[k, 1, pl.ds(pl.multiple_of(8 * me, 8), 8), :] = im

    translate(me, put_own)

    get_phi_b.wait()
    hi, lo = split(phi_b[...])
    azi[0:128, :] = hi
    azi[128:256, :] = hi
    azi[256:384, :] = lo
    get_shift_c.wait()
    upper_half = core == 0
    for o in range(8):
        pair = MERGE * jnp.concatenate(cos_sin(shift_c[o]), 1)
        four = jnp.where(upper_half, pair[0:4], pair[4:8])
        cs[o] = jnp.concatenate([four] * 4, 0)
    get_pmap.wait()
    owner = onehot(iota((16, 128), 0) == pmap[...])
    rep_p = onehot(iota((256, 16), 1) == iota((256, 16), 0) // 16)
    owner_rows = dot(rep_p, owner).astype(BF16)
    same = iota((256, 256), 0) % 16 == iota((256, 256), 1) % 16
    box = iota((128, 256), 0)
    slot = iota((128, 256), 1) // 16
    total[...] = jnp.zeros_like(total)
    all_b.wait_recv()

    @pl.loop(0, 8)
    def _(o):
        pick_box = onehot(box == 8 * slot + o)
        pick = jnp.where(same, dot(owner_rows, pick_box), 0.0).astype(BF16)
        rows = [
            jnp.concatenate([recv_b[8 * m + o, 0], recv_b[8 * m + o, 1]], 1) for m in range(16)
        ]
        hi, lo = split(jnp.concatenate(rows, 0))
        merged = dot(jnp.concatenate([pick, pick], 1), jnp.concatenate([hi, lo], 0))
        cosine, sine = cs[o, :, 0:256], cs[o, :, 256:512]
        group[0:256, :] = merged[:, 0:128]
        group[256:512, :] = merged[:, 128:256]
        for h in range(2):
            parts = []
            for c in range(2):
                hi, lo = split(group[256 * c + 128 * h : 256 * c + 128 * h + 128, :])
                parts.append(
                    dot(jnp.concatenate([hi, lo, hi], 1), azi[...]).reshape(8, 16, 256)
                )
            re, im = parts
            for c, turned in enumerate(
                (cosine * re - sine * im, sine * re + cosine * im)
            ):
                total[pl.ds(8 * h, 8), c] += turned

    for i in range(4):
        parents_ref[:, :, i] = total[:, :, 4 * i : 4 * i + 4, :]

    all_c.wait_recv()
    for k in range(4):
        for c in range(2):
            for i in range(4):
                incoming_ref[k, c, i] = recv_c[k, c, pl.ds(i, 64, stride=4), :]
    all_a.wait_send()
    all_b.wait_send()
    all_c.wait_send()


def on_device(
    leaves, theta_a, phi_a, shift_b, theta_b, phi_b, shift_c, parent_map, inter_list, op_index,
    trans_ops,
):
    grid = leaves.reshape(32, 2, 4, 16, 128).transpose(0, 1, 3, 2, 4).reshape(32, 2, 64, 128)
    hbm = pl.BlockSpec(memory_space=pltpu.HBM)
    vmem = pl.BlockSpec(memory_space=pltpu.VMEM)

    def v(*shape, kind=F32):
        return pltpu.VMEM(shape, kind)

    dma = pltpu.SemaphoreType.DMA
    return pl.pallas_call(
        kernel,
        out_shape=(
            jax.ShapeDtypeStruct((16, 2, 4, 4, 256), F32),
            jax.ShapeDtypeStruct((4, 2, 4, 64, 128), F32),
        ),
        in_specs=[hbm] * 11,
        out_specs=(vmem, vmem),
        scratch_shapes=[
            v(32, 2, 64, 128), v(32, 64), v(64, 128), v(8, 64, 128), v(64, 128), v(128, 256),
            v(8, 8, 256), v(1, 128, kind=jnp.int32),
            pltpu.SMEM((LIST, 128), jnp.int32), pltpu.SMEM((LIST, 128), jnp.int32),
            v(2, NOPS, 2, 128),
            v(384, 256, kind=BF16), v(256, 384, kind=BF16), v(512, 768, kind=BF16),
            v(8, 256, 256), v(256, 256), v(NOPS, 2, 8, 128), v(8, 16, 512),
            v(4, 32, 2, 8, 128), v(128, 2, 8, 128),
            v(4, 32, 2, 16, 128), v(128, 2, 16, 128),
            v(32, 4, 2, 8, 128), v(4, 2, 256, 128),
            v(384, 256, kind=BF16), v(512, 128), v(16, 2, 16, 256),
            dma((10,)), dma((4,)), dma, dma, dma, dma, dma, dma,
        ],
        compiler_params=pltpu.CompilerParams(
            collective_id=0, has_side_effects=True, vmem_limit_bytes=48 * 2**20
        ),
    )(
        grid, theta_a, phi_a, shift_b, theta_b, phi_b, shift_c, parent_map.reshape(1, 128),
        inter_list.T, op_index.T, trans_ops,
    )


def solution(mesh):
    r = P()
    in_specs = (P("box", None, "inc", None),) + (r,) * 9 + (P(None, None, "box", None),)
    out_specs = (P(None, None, "inc", "box", None), P("box", None, "inc", None, None))
    return jax.shard_map(
        on_device, mesh=mesh, in_specs=in_specs, out_specs=out_specs, check_vma=False
    )
```

```python
import functools

import jax
import jax.numpy as jnp
from jax import lax
from jax.experimental import pallas as pl
from jax.experimental.pallas import tpu as pltpu
from jax.sharding import PartitionSpec as P

F32 = jnp.float32
BF16 = jnp.bfloat16
MESH = pl.DeviceIdType.MESH
N = 32
NOPS = 316
LIST = 32
MERGE = 0.35

HOPS = (
    (2, 2),
    (2, 1), (2, 3), (1, 2), (3, 2),
    (0, 2), (2, 0),
    (1, 3), (3, 1),
    (1, 1), (3, 3),
    (0, 1), (0, 3), (1, 0), (3, 0),
)


def dot(a, b):
    return lax.dot_general(a, b, (((1,), (0,)), ((), ())), preferred_element_type=F32)


def dot_t(a, b):
    return lax.dot_general(a, b, (((0,), (0,)), ((), ())), preferred_element_type=F32)


def split(x):
    hi = x.astype(BF16)
    lo = (x - hi.astype(F32)).astype(BF16)
    return hi, lo


def split3(x):
    hi = x.astype(BF16)
    rest = x - hi.astype(F32)
    mid = rest.astype(BF16)
    lo = (rest - mid.astype(F32)).astype(BF16)
    return hi, mid, lo


def cos_sin(angle):
    h = angle * 0.5
    g = h * h
    s = 1.0 / 6227020800.0
    for c in (-1.0 / 39916800.0, 1.0 / 362880.0, -1.0 / 5040.0, 1.0 / 120.0, -1.0 / 6.0, 1.0):
        s = s * g + c
    s = s * h
    c0 = 1.0 / 479001600.0
    for c in (-1.0 / 3628800.0, 1.0 / 40320.0, -1.0 / 720.0, 1.0 / 24.0, -0.5, 1.0):
        c0 = c0 * g + c
    return 1.0 - 2.0 * s * s, 2.0 * s * c0


def iota(shape, dim):
    return lax.broadcasted_iota(jnp.int32, shape, dim)


def onehot(cond):
    return jnp.where(cond, 1.0, 0.0).astype(F32).astype(BF16)


def kernel(
    leaves_hbm, theta_a_hbm, phi_a_hbm, shift_b_hbm, theta_b_hbm, phi_b_hbm, shift_c_hbm,
    pmap_hbm, list_hbm, ops_hbm, trans_hbm,
    parents_ref, incoming_ref,
    leaves, theta_a, phi_a, shift_b, theta_b, phi_b, shift_c, pmap, ilist, iops, trans,
    q3, w3, v3, tab, middle, gains, cs,
    buf_a, recv_a, buf_b, recv_b, buf_c, recv_c, azi, group, total,
    in_sem, leaf_sem, send_a, got_a, send_b, got_b, send_c, got_c,
):
    me = lax.axis_index("box")
    z, x, core = me // 8, (me // 2) % 4, me % 2
    zs = [((z + k) % 4) * 8 for k in range(4)]
    xs = [((x + k) % 4) * 2 for k in range(4)]
    cores = [core, 1 - core]
    partners = [zs[dz] + xs[dx] + cores[dc] for dz, dx in HOPS for dc in range(2)]
    partners.append(zs[0] + xs[0] + cores[1])

    barrier = pltpu.get_barrier_semaphore()
    for d in partners:
        pl.semaphore_signal(barrier, inc=1, device_id={"box": d}, device_id_type=MESH)

    def fetch(k, src, dst):
        copy = pltpu.make_async_copy(src, dst, in_sem.at[k])
        copy.start()
        return copy

    get_theta_a = fetch(0, theta_a_hbm, theta_a)
    get_phi_a = fetch(1, phi_a_hbm, phi_a)
    get_leaves = []
    for q in range(4):
        copy = pltpu.make_async_copy(
            leaves_hbm.at[pl.ds(8 * q, 8)], leaves.at[pl.ds(8 * q, 8)], leaf_sem.at[q]
        )
        copy.start()
        get_leaves.append(copy)
    get_shift_b = fetch(2, shift_b_hbm, shift_b)
    get_theta_b = fetch(3, theta_b_hbm, theta_b)
    get_trans = fetch(4, trans_hbm, trans)
    get_list = fetch(5, list_hbm, ilist)
    get_ops = fetch(6, ops_hbm, iops)
    get_phi_b = fetch(7, phi_b_hbm, phi_b)
    get_pmap = fetch(8, pmap_hbm, pmap)
    get_shift_c = fetch(
        9, shift_c_hbm.at[:, pl.ds(pl.multiple_of(8 * (me // 2), 8), 8), :], shift_c
    )

    get_phi_a.wait()
    for i, half in enumerate(split(phi_a[...])):
        none = jnp.zeros_like(half)
        both = jnp.concatenate(
            [jnp.concatenate([half, none], 1), jnp.concatenate([none, half], 1)], 0
        )
        if i == 0:
            q3[0:128, :] = both
            q3[128:256, :] = both
        else:
            q3[256:384, :] = both

    get_theta_a.wait()
    col = iota((32, 128), 1)
    pick_t = onehot(iota((32, 128), 0) == 2 * ((col % 64) // 4) + col // 64)
    rep_u = onehot(iota((256, 64), 1) == iota((256, 64), 0) // 4)
    same = iota((256, 128), 0) % 4 == iota((256, 128), 1) % 4
    for i, half in enumerate(split(theta_a[...])):
        wide = dot(rep_u, dot_t(half, pick_t).astype(BF16))
        wide = jnp.where(same, wide, 0.0).astype(BF16)
        if i == 0:
            w3[:, 0:128] = wide
            w3[:, 256:384] = wide
        else:
            w3[:, 128:256] = wide

    get_shift_b.wait()
    rep_u3 = jnp.concatenate([rep_u, rep_u, rep_u], 1)

    @pl.loop(0, 8)
    def _(o):
        cosine, sine = cos_sin(shift_b[o])
        pair = MERGE * jnp.concatenate([cosine, sine], 1)
        tab[o] = dot(rep_u3, jnp.concatenate(split3(pair), 0))

    def middle_matrix():
        get_theta_b.wait()
        pick_u = onehot(iota((64, 256), 0) == iota((64, 256), 1) // 4)
        row = iota((512, 128), 0)
        rep_u2 = onehot(iota((512, 128), 1) == 4 * (row // 16) + row % 4)
        same = (iota((512, 256), 0) % 16) // 4 == iota((512, 256), 1) % 4
        for i, half in enumerate(split(theta_b[...])):
            wide = dot(rep_u2, dot_t(half, pick_u).astype(BF16))
            wide = jnp.where(same, wide, 0.0).astype(BF16)
            if i == 0:
                v3[:, 0:256] = wide
                v3[:, 512:768] = wide
            else:
                v3[:, 256:512] = wide

    def merge(q):
        def one_leaf(o):
            pattern = leaves[8 * q + o].reshape(128, 128)
            hi, lo = split(pattern)
            y = dot(jnp.concatenate([hi, lo, hi], 1), q3[...])
            y = jnp.concatenate(
                [
                    jnp.concatenate([y[0:64, 0:128], y[64:128, 0:128]], 1),
                    jnp.concatenate([y[0:64, 128:256], y[64:128, 128:256]], 1),
                ],
                0,
            )
            hi, lo = split(y)
            up = dot(w3[...], jnp.concatenate([hi, hi, lo], 0))
            cosine, sine = tab[o, :, 0:128], tab[o, :, 128:256]
            re, im = up[:, 0:128], up[:, 128:256]
            middle[q, :, 0:128] += cosine * re - sine * im
            middle[q, :, 128:256] += sine * re + cosine * im

        middle[q] = jnp.zeros((256, 256), F32)
        for o in range(8):
            one_leaf(o)
        for c in range(2):
            buf_a[q, :, c] = middle[q, :, 128 * c : 128 * c + 128].reshape(32, 8, 128)
        recv_a[4 * me + q] = buf_a[q, me]

    def raise_polar(q):
        hi, lo = split(middle[q])
        polar = dot(v3[...], jnp.concatenate([hi, hi, lo], 0))
        for c in range(2):
            buf_b[q, :, c] = polar[:, 128 * c : 128 * c + 128].reshape(32, 16, 128)
        recv_b[4 * me + q] = buf_b[q, me]

    def send(q, buf, recv, send_sem, got_sem):
        for d in partners:
            pltpu.make_async_remote_copy(
                src_ref=buf.at[q, d],
                dst_ref=recv.at[4 * me + q],
                send_sem=send_sem,
                recv_sem=got_sem,
                device_id={"box": d},
                device_id_type=MESH,
            ).start()

    def send_rows(q):
        send(q, buf_a, recv_a, send_a, got_a)

    def send_polar(q):
        send(q, buf_b, recv_b, send_b, got_b)

    get_leaves[0].wait()
    merge(0)
    pl.semaphore_wait(barrier, N - 1)
    send_rows(0)
    middle_matrix()
    raise_polar(0)
    send_polar(0)
    for q in range(1, 4):
        get_leaves[q].wait()

    @pl.loop(1, 4)
    def _(q):
        merge(q)
        send_rows(q)

    @pl.loop(1, 4)
    def _(q):
        raise_polar(q)
        send_polar(q)

    get_trans.wait()
    upper = iota((8, 128), 0) < 4

    @pl.loop(0, NOPS // 4)
    def _(k):
        for j in range(4):
            for c in range(2):
                two = trans[c, 4 * k + j]
                gains[4 * k + j, c] = jnp.where(
                    upper,
                    jnp.broadcast_to(two[0:1], (8, 128)),
                    jnp.broadcast_to(two[1:2], (8, 128)),
                )

    def every(ref, send_sem, got_sem):
        return pltpu.make_async_remote_copy(
            src_ref=ref,
            dst_ref=ref,
            send_sem=send_sem,
            recv_sem=got_sem,
            device_id={"box": partners[-1]},
            device_id_type=MESH,
        )

    all_a = every(recv_a.at[pl.ds(0, 124)], send_a, got_a)
    all_b = every(recv_b.at[pl.ds(0, 124)], send_b, got_b)
    all_c = every(recv_c.at[:, :, pl.ds(0, 248), :], send_c, got_c)
    get_list.wait()
    get_ops.wait()
    all_a.wait_recv()

    def translate(d, put):
        @pl.loop(0, 4)
        def _(k):
            t = 4 * d + k
            sums = [jnp.zeros((8, 128), F32) for _ in range(4)]
            for j in range(LIST):
                s, o = ilist[j, t], iops[j, t]
                sr, si = recv_a[s, 0], recv_a[s, 1]
                gr, gi = gains[o, 0], gains[o, 1]
                sums[0] += gr * sr
                sums[1] += gi * si
                sums[2] += gr * si
                sums[3] += gi * sr
            put(k, sums[0] - sums[1], sums[2] + sums[3])

    for d in partners:

        def put(k, re, im, d=d):
            buf_c[d, k, 0] = re
            buf_c[d, k, 1] = im

        translate(d, put)
        pltpu.make_async_remote_copy(
            src_ref=buf_c.at[d],
            dst_ref=recv_c.at[:, :, pl.ds(pl.multiple_of(8 * me, 8), 8), :],
            send_sem=send_c,
            recv_sem=got_c,
            device_id={"box": d},
            device_id_type=MESH,
        ).start()

    def put_own(k, re, im):
        recv_c[k, 0, pl.ds(pl.multiple_of(8 * me, 8), 8), :] = re
        recv_c[k, 1, pl.ds(pl.multiple_of(8 * me, 8), 8), :] = im

    translate(me, put_own)

    get_phi_b.wait()
    hi, lo = split(phi_b[...])
    azi[0:128, :] = hi
    azi[128:256, :] = hi
    azi[256:384, :] = lo
    get_shift_c.wait()
    upper_half = core == 0
    for o in range(8):
        pair = MERGE * jnp.concatenate(cos_sin(shift_c[o]), 1)
        four = jnp.where(upper_half, pair[0:4], pair[4:8])
        cs[o] = jnp.concatenate([four] * 4, 0)
    get_pmap.wait()
    owner = onehot(iota((16, 128), 0) == pmap[...])
    rep_p = onehot(iota((256, 16), 1) == iota((256, 16), 0) // 16)
    owner_rows = dot(rep_p, owner).astype(BF16)
    same = iota((256, 256), 0) % 16 == iota((256, 256), 1) % 16
    box = iota((128, 256), 0)
    slot = iota((128, 256), 1) // 16
    total[...] = jnp.zeros_like(total)
    all_b.wait_recv()

    @pl.loop(0, 8)
    def _(o):
        pick_box = onehot(box == 8 * slot + o)
        pick = jnp.where(same, dot(owner_rows, pick_box), 0.0).astype(BF16)
        rows = [
            jnp.concatenate([recv_b[8 * m + o, 0], recv_b[8 * m + o, 1]], 1) for m in range(16)
        ]
        hi, lo = split(jnp.concatenate(rows, 0))
        merged = dot(jnp.concatenate([pick, pick], 1), jnp.concatenate([hi, lo], 0))
        cosine, sine = cs[o, :, 0:256], cs[o, :, 256:512]
        group[0:256, :] = merged[:, 0:128]
        group[256:512, :] = merged[:, 128:256]
        for h in range(2):
            parts = []
            for c in range(2):
                hi, lo = split(group[256 * c + 128 * h : 256 * c + 128 * h + 128, :])
                parts.append(
                    dot(jnp.concatenate([hi, lo, hi], 1), azi[...]).reshape(8, 16, 256)
                )
            re, im = parts
            for c, turned in enumerate(
                (cosine * re - sine * im, sine * re + cosine * im)
            ):
                total[pl.ds(8 * h, 8), c] += turned

    for i in range(4):
        parents_ref[:, :, i] = total[:, :, 4 * i : 4 * i + 4, :]

    all_c.wait_recv()
    for k in range(4):
        for c in range(2):
            for i in range(4):
                incoming_ref[k, c, i] = recv_c[k, c, pl.ds(i, 64, stride=4), :]
    all_a.wait_send()
    all_b.wait_send()
    all_c.wait_send()


def on_device(
    leaves, theta_a, phi_a, shift_b, theta_b, phi_b, shift_c, parent_map, inter_list, op_index,
    trans_ops,
):
    grid = leaves.reshape(32, 2, 4, 16, 128).transpose(0, 1, 3, 2, 4).reshape(32, 2, 64, 128)
    hbm = pl.BlockSpec(memory_space=pltpu.HBM)
    vmem = pl.BlockSpec(memory_space=pltpu.VMEM)

    def v(*shape, kind=F32):
        return pltpu.VMEM(shape, kind)

    dma = pltpu.SemaphoreType.DMA
    return pl.pallas_call(
        kernel,
        out_shape=(
            pltpu.VMEM((16, 2, 4, 4, 256), F32),
            pltpu.VMEM((4, 2, 4, 64, 128), F32),
        ),
        in_specs=[hbm] * 11,
        out_specs=(vmem, vmem),
        scratch_shapes=[
            v(32, 2, 64, 128), v(32, 64), v(64, 128), v(8, 64, 128), v(64, 128), v(128, 256),
            v(8, 8, 256), v(1, 128, kind=jnp.int32),
            pltpu.SMEM((LIST, 128), jnp.int32), pltpu.SMEM((LIST, 128), jnp.int32),
            v(2, NOPS, 2, 128),
            v(384, 256, kind=BF16), v(256, 384, kind=BF16), v(512, 768, kind=BF16),
            v(8, 256, 256), v(4, 256, 256), v(NOPS, 2, 8, 128), v(8, 16, 512),
            v(4, 32, 2, 8, 128), v(128, 2, 8, 128),
            v(4, 32, 2, 16, 128), v(128, 2, 16, 128),
            v(32, 4, 2, 8, 128), v(4, 2, 256, 128),
            v(384, 256, kind=BF16), v(512, 128), v(16, 2, 16, 256),
            dma((10,)), dma((4,)), dma, dma, dma, dma, dma, dma,
        ],
        compiler_params=pltpu.CompilerParams(
            collective_id=0, has_side_effects=True, vmem_limit_bytes=56 * 2**20
        ),
    )(
        grid, theta_a, phi_a, shift_b, theta_b, phi_b, shift_c, parent_map.reshape(1, 128),
        inter_list.T, op_index.T, trans_ops,
    )


def solution(mesh):
    r = P()
    in_specs = (P("box", None, "inc", None),) + (r,) * 9 + (P(None, None, "box", None),)
    out_specs = (P(None, None, "inc", "box", None), P("box", None, "inc", None, None))
    return jax.shard_map(
        on_device, mesh=mesh, in_specs=in_specs, out_specs=out_specs, check_vma=False
    )
```

```python
import functools

import jax
import jax.numpy as jnp
from jax import lax
from jax.experimental import pallas as pl
from jax.experimental.pallas import tpu as pltpu
from jax.sharding import PartitionSpec as P

F32 = jnp.float32
BF16 = jnp.bfloat16
MESH = pl.DeviceIdType.MESH
N = 32
NOPS = 316
LIST = 32
MERGE = 0.35

HOPS = (
    (2, 2),
    (2, 1), (2, 3), (1, 2), (3, 2),
    (0, 2), (2, 0),
    (1, 3), (3, 1),
    (1, 1), (3, 3),
    (0, 1), (0, 3), (1, 0), (3, 0),
)


def dot(a, b):
    return lax.dot_general(a, b, (((1,), (0,)), ((), ())), preferred_element_type=F32)


def dot_t(a, b):
    return lax.dot_general(a, b, (((0,), (0,)), ((), ())), preferred_element_type=F32)


def split(x):
    hi = x.astype(BF16)
    lo = (x - hi.astype(F32)).astype(BF16)
    return hi, lo


def split3(x):
    hi = x.astype(BF16)
    rest = x - hi.astype(F32)
    mid = rest.astype(BF16)
    lo = (rest - mid.astype(F32)).astype(BF16)
    return hi, mid, lo


def cos_sin(angle):
    h = angle * 0.5
    g = h * h
    s = 1.0 / 6227020800.0
    for c in (-1.0 / 39916800.0, 1.0 / 362880.0, -1.0 / 5040.0, 1.0 / 120.0, -1.0 / 6.0, 1.0):
        s = s * g + c
    s = s * h
    c0 = 1.0 / 479001600.0
    for c in (-1.0 / 3628800.0, 1.0 / 40320.0, -1.0 / 720.0, 1.0 / 24.0, -0.5, 1.0):
        c0 = c0 * g + c
    return 1.0 - 2.0 * s * s, 2.0 * s * c0


def iota(shape, dim):
    return lax.broadcasted_iota(jnp.int32, shape, dim)


def onehot(cond):
    return jnp.where(cond, 1.0, 0.0).astype(F32).astype(BF16)


def kernel(
    leaves_hbm, theta_a_hbm, phi_a_hbm, shift_b_hbm, theta_b_hbm, phi_b_hbm, shift_c_hbm,
    pmap_hbm, list_hbm, ops_hbm, trans_hbm,
    parents_ref, recv_c,
    leaves, theta_a, phi_a, shift_b, theta_b, phi_b, shift_c, pmap, ilist, iops, trans,
    q3, w3, v3, tab, middle, gains, cs,
    buf_a, recv_a, buf_b, recv_b, buf_c, azi, group, total,
    in_sem, leaf_sem, send_a, got_a, send_b, got_b, send_c, got_c,
):
    me = lax.axis_index("box")
    z, x, core = me // 8, (me // 2) % 4, me % 2
    zs = [((z + k) % 4) * 8 for k in range(4)]
    xs = [((x + k) % 4) * 2 for k in range(4)]
    cores = [core, 1 - core]
    partners = [zs[dz] + xs[dx] + cores[dc] for dz, dx in HOPS for dc in range(2)]
    partners.append(zs[0] + xs[0] + cores[1])

    def fetch(k, src, dst):
        copy = pltpu.make_async_copy(src, dst, in_sem.at[k])
        copy.start()
        return copy

    def fetch_leaves(q):
        copy = pltpu.make_async_copy(
            leaves_hbm.at[pl.ds(8 * q, 8)], leaves.at[pl.ds(8 * q, 8)], leaf_sem.at[q]
        )
        copy.start()
        return copy

    get_shift_b = fetch(2, shift_b_hbm, shift_b)
    get_phi_a = fetch(1, phi_a_hbm, phi_a)
    get_theta_a = fetch(0, theta_a_hbm, theta_a)
    get_leaves = [fetch_leaves(0)]

    barrier = pltpu.get_barrier_semaphore()
    for d in partners:
        pl.semaphore_signal(barrier, inc=1, device_id={"box": d}, device_id_type=MESH)

    get_theta_b = fetch(3, theta_b_hbm, theta_b)
    get_leaves += [fetch_leaves(q) for q in range(1, 4)]
    get_trans = fetch(4, trans_hbm, trans)
    get_list = fetch(5, list_hbm, ilist)
    get_ops = fetch(6, ops_hbm, iops)
    get_phi_b = fetch(7, phi_b_hbm, phi_b)
    get_pmap = fetch(8, pmap_hbm, pmap)
    get_shift_c = fetch(
        9, shift_c_hbm.at[:, pl.ds(pl.multiple_of(8 * (me // 2), 8), 8), :], shift_c
    )

    get_phi_a.wait()
    for i, half in enumerate(split(phi_a[...])):
        none = jnp.zeros_like(half)
        both = jnp.concatenate(
            [jnp.concatenate([half, none], 1), jnp.concatenate([none, half], 1)], 0
        )
        if i == 0:
            q3[0:128, :] = both
            q3[128:256, :] = both
        else:
            q3[256:384, :] = both

    get_theta_a.wait()
    col = iota((32, 128), 1)
    pick_t = onehot(iota((32, 128), 0) == 2 * ((col % 64) // 4) + col // 64)
    rep_u = onehot(iota((256, 64), 1) == iota((256, 64), 0) // 4)
    same = iota((256, 128), 0) % 4 == iota((256, 128), 1) % 4
    for i, half in enumerate(split(theta_a[...])):
        wide = dot(rep_u, dot_t(half, pick_t).astype(BF16))
        wide = jnp.where(same, wide, 0.0).astype(BF16)
        if i == 0:
            w3[:, 0:128] = wide
            w3[:, 256:384] = wide
        else:
            w3[:, 128:256] = wide

    get_shift_b.wait()
    rep_u3 = jnp.concatenate([rep_u, rep_u, rep_u], 1)

    @pl.loop(0, 8, unroll=True)
    def _(o):
        cosine, sine = cos_sin(shift_b[o])
        pair = MERGE * jnp.concatenate([cosine, sine], 1)
        tab[o] = dot(rep_u3, jnp.concatenate(split3(pair), 0))

    def middle_matrix():
        get_theta_b.wait()
        pick_u = onehot(iota((64, 256), 0) == iota((64, 256), 1) // 4)
        row = iota((512, 128), 0)
        rep_u2 = onehot(iota((512, 128), 1) == 4 * (row // 16) + row % 4)
        same = (iota((512, 256), 0) % 16) // 4 == iota((512, 256), 1) % 4
        for i, half in enumerate(split(theta_b[...])):
            wide = dot(rep_u2, dot_t(half, pick_u).astype(BF16))
            wide = jnp.where(same, wide, 0.0).astype(BF16)
            if i == 0:
                v3[:, 0:256] = wide
                v3[:, 512:768] = wide
            else:
                v3[:, 256:512] = wide

    def merge(q):
        def one_leaf(o):
            pattern = leaves[8 * q + o].reshape(128, 128)
            hi, lo = split(pattern)
            y = dot(jnp.concatenate([hi, lo, hi], 1), q3[...])
            y = jnp.concatenate(
                [
                    jnp.concatenate([y[0:64, 0:128], y[64:128, 0:128]], 1),
                    jnp.concatenate([y[0:64, 128:256], y[64:128, 128:256]], 1),
                ],
                0,
            )
            hi, lo = split(y)
            up = dot(w3[...], jnp.concatenate([hi, hi, lo], 0))
            cosine, sine = tab[o, :, 0:128], tab[o, :, 128:256]
            re, im = up[:, 0:128], up[:, 128:256]
            middle[q, :, 0:128] += cosine * re - sine * im
            middle[q, :, 128:256] += sine * re + cosine * im

        middle[q] = jnp.zeros((256, 256), F32)
        for o in range(8):
            one_leaf(o)
        for c in range(2):
            buf_a[q, :, c] = middle[q, :, 128 * c : 128 * c + 128].reshape(32, 8, 128)
        recv_a[4 * me + q] = buf_a[q, me]

    def raise_polar(q):
        hi, lo = split(middle[q])
        polar = dot(v3[...], jnp.concatenate([hi, hi, lo], 0))
        for c in range(2):
            buf_b[q, :, c] = polar[:, 128 * c : 128 * c + 128].reshape(32, 16, 128)
        recv_b[4 * me + q] = buf_b[q, me]

    def send(q, buf, recv, send_sem, got_sem):
        for d in partners:
            pltpu.make_async_remote_copy(
                src_ref=buf.at[q, d],
                dst_ref=recv.at[4 * me + q],
                send_sem=send_sem,
                recv_sem=got_sem,
                device_id={"box": d},
                device_id_type=MESH,
            ).start()

    def send_rows(q):
        send(q, buf_a, recv_a, send_a, got_a)

    def send_polar(q):
        send(q, buf_b, recv_b, send_b, got_b.at[q])

    get_leaves[0].wait()
    merge(0)
    pl.semaphore_wait(barrier, N - 1)
    send_rows(0)
    middle_matrix()
    raise_polar(0)
    send_polar(0)
    for q in range(1, 4):
        get_leaves[q].wait()

    @pl.loop(1, 4)
    def _(q):
        merge(q)
        send_rows(q)

    @pl.loop(1, 4)
    def _(q):
        raise_polar(q)
        send_polar(q)

    get_trans.wait()
    upper = iota((8, 128), 0) < 4

    @pl.loop(0, NOPS // 4)
    def _(k):
        for j in range(4):
            for c in range(2):
                two = trans[c, 4 * k + j]
                gains[4 * k + j, c] = jnp.where(
                    upper,
                    jnp.broadcast_to(two[0:1], (8, 128)),
                    jnp.broadcast_to(two[1:2], (8, 128)),
                )

    def every(ref, send_sem, got_sem):
        return pltpu.make_async_remote_copy(
            src_ref=ref,
            dst_ref=ref,
            send_sem=send_sem,
            recv_sem=got_sem,
            device_id={"box": partners[-1]},
            device_id_type=MESH,
        )

    all_a = every(recv_a.at[pl.ds(0, 124)], send_a, got_a)
    sent_b = every(buf_b.at[:, pl.ds(0, 31)], send_b, got_b.at[0])
    rounds_b = [every(buf_b.at[0, pl.ds(0, 31)], send_b, got_b.at[q]) for q in range(4)]
    all_c = every(recv_c.at[:, :, pl.ds(0, 248), :], send_c, got_c)
    get_list.wait()
    get_ops.wait()
    all_a.wait_recv()

    def translate(d, put):
        @pl.loop(0, 4)
        def _(k):
            t = 4 * d + k
            sums = [jnp.zeros((8, 128), F32) for _ in range(4)]
            for j in range(LIST):
                s, o = ilist[j, t], iops[j, t]
                sr, si = recv_a[s, 0], recv_a[s, 1]
                gr, gi = gains[o, 0], gains[o, 1]
                sums[0] += gr * sr
                sums[1] += gi * si
                sums[2] += gr * si
                sums[3] += gi * sr
            put(k, sums[0] - sums[1], sums[2] + sums[3])

    for d in partners:

        def put(k, re, im, d=d):
            buf_c[d, k, 0] = re
            buf_c[d, k, 1] = im

        translate(d, put)
        pltpu.make_async_remote_copy(
            src_ref=buf_c.at[d],
            dst_ref=recv_c.at[:, :, pl.ds(pl.multiple_of(8 * me, 8), 8), :],
            send_sem=send_c,
            recv_sem=got_c,
            device_id={"box": d},
            device_id_type=MESH,
        ).start()

    def put_own(k, re, im):
        recv_c[k, 0, pl.ds(pl.multiple_of(8 * me, 8), 8), :] = re
        recv_c[k, 1, pl.ds(pl.multiple_of(8 * me, 8), 8), :] = im

    translate(me, put_own)

    get_phi_b.wait()
    hi, lo = split(phi_b[...])
    azi[0:128, :] = hi
    azi[128:256, :] = hi
    azi[256:384, :] = lo
    get_shift_c.wait()
    upper_half = core == 0
    for o in range(8):
        pair = MERGE * jnp.concatenate(cos_sin(shift_c[o]), 1)
        four = jnp.where(upper_half, pair[0:4], pair[4:8])
        cs[o] = jnp.concatenate([four] * 4, 0)
    get_pmap.wait()
    owner = onehot(iota((16, 128), 0) == pmap[...])
    rep_p = onehot(iota((256, 16), 1) == iota((256, 16), 0) // 16)
    owner_rows = dot(rep_p, owner).astype(BF16)
    same = iota((256, 256), 0) % 16 == iota((256, 256), 1) % 16
    box = iota((128, 256), 0)
    slot = iota((128, 256), 1) // 16
    total[...] = jnp.zeros_like(total)

    def merge_octant(o):
        pick_box = onehot(box == 8 * slot + o)
        pick = jnp.where(same, dot(owner_rows, pick_box), 0.0).astype(BF16)
        rows = [
            jnp.concatenate([recv_b[8 * m + o, 0], recv_b[8 * m + o, 1]], 1) for m in range(16)
        ]
        hi, lo = split(jnp.concatenate(rows, 0))
        merged = dot(jnp.concatenate([pick, pick], 1), jnp.concatenate([hi, lo], 0))
        cosine, sine = cs[o, :, 0:256], cs[o, :, 256:512]
        group[0:256, :] = merged[:, 0:128]
        group[256:512, :] = merged[:, 128:256]
        for h in range(2):
            parts = []
            for c in range(2):
                hi, lo = split(group[256 * c + 128 * h : 256 * c + 128 * h + 128, :])
                parts.append(
                    dot(jnp.concatenate([hi, lo, hi], 1), azi[...]).reshape(8, 16, 256)
                )
            re, im = parts
            for c, turned in enumerate(
                (cosine * re - sine * im, sine * re + cosine * im)
            ):
                total[pl.ds(8 * h, 8), c] += turned

    for q in range(4):
        rounds_b[q].wait_recv()
        merge_octant(q)
        merge_octant(q + 4)

    for i in range(4):
        parents_ref[:, :, i] = total[:, :, 4 * i : 4 * i + 4, :]

    all_c.wait_recv()
    all_a.wait_send()
    sent_b.wait_send()
    all_c.wait_send()


def write(parents_in, rows_in, parents_hbm, incoming_hbm, rows, sem):
    copies = [pltpu.make_async_copy(parents_in, parents_hbm, sem.at[4])]
    copies[0].start()
    for k in range(4):
        for c in range(2):
            for i in range(4):
                rows[k, c, i] = rows_in[k, c, pl.ds(i, 64, stride=4), :]
        copies.append(pltpu.make_async_copy(rows.at[k], incoming_hbm.at[k], sem.at[k]))
        copies[-1].start()
    for copy in copies:
        copy.wait()


def on_device(
    leaves, theta_a, phi_a, shift_b, theta_b, phi_b, shift_c, parent_map, inter_list, op_index,
    trans_ops,
):
    grid = leaves.reshape(32, 2, 4, 16, 128).transpose(0, 1, 3, 2, 4).reshape(32, 2, 64, 128)
    hbm = pl.BlockSpec(memory_space=pltpu.HBM)
    vmem = pl.BlockSpec(memory_space=pltpu.VMEM)

    def v(*shape, kind=F32):
        return pltpu.VMEM(shape, kind)

    dma = pltpu.SemaphoreType.DMA
    parents, rows = pl.pallas_call(
        kernel,
        out_shape=(
            pltpu.VMEM((16, 2, 4, 4, 256), F32),
            pltpu.VMEM((4, 2, 256, 128), F32),
        ),
        in_specs=[hbm] * 11,
        out_specs=(vmem, vmem),
        scratch_shapes=[
            v(32, 2, 64, 128), v(32, 64), v(64, 128), v(8, 64, 128), v(64, 128), v(128, 256),
            v(8, 8, 256), v(1, 128, kind=jnp.int32),
            pltpu.SMEM((LIST, 128), jnp.int32), pltpu.SMEM((LIST, 128), jnp.int32),
            v(2, NOPS, 2, 128),
            v(384, 256, kind=BF16), v(256, 384, kind=BF16), v(512, 768, kind=BF16),
            v(8, 256, 256), v(4, 256, 256), v(NOPS, 2, 8, 128), v(8, 16, 512),
            v(4, 32, 2, 8, 128), v(128, 2, 8, 128),
            v(4, 32, 2, 16, 128), v(128, 2, 16, 128),
            v(32, 4, 2, 8, 128),
            v(384, 256, kind=BF16), v(512, 128), v(16, 2, 16, 256),
            dma((10,)), dma((4,)), dma, dma, dma, dma((4,)), dma, dma,
        ],
        compiler_params=pltpu.CompilerParams(
            collective_id=0, has_side_effects=True, vmem_limit_bytes=56 * 2**20
        ),
    )(
        grid, theta_a, phi_a, shift_b, theta_b, phi_b, shift_c, parent_map.reshape(1, 128),
        inter_list.T, op_index.T, trans_ops,
    )
    return pl.pallas_call(
        write,
        out_shape=(
            jax.ShapeDtypeStruct((16, 2, 4, 4, 256), F32),
            jax.ShapeDtypeStruct((4, 2, 4, 64, 128), F32),
        ),
        in_specs=[vmem, vmem],
        out_specs=(hbm, hbm),
        scratch_shapes=[v(4, 2, 4, 64, 128), dma((5,))],
        compiler_params=pltpu.CompilerParams(vmem_limit_bytes=8 * 2**20),
    )(parents, rows)


def solution(mesh):
    r = P()
    in_specs = (P("box", None, "inc", None),) + (r,) * 9 + (P(None, None, "box", None),)
    out_specs = (P(None, None, "inc", "box", None), P("box", None, "inc", None, None))
    return jax.shard_map(
        on_device, mesh=mesh, in_specs=in_specs, out_specs=out_specs, check_vma=False
    )
```

```python
import functools

import jax
import jax.numpy as jnp
from jax import lax
from jax.experimental import pallas as pl
from jax.experimental.pallas import tpu as pltpu
from jax.sharding import PartitionSpec as P

F32 = jnp.float32
BF16 = jnp.bfloat16
MESH = pl.DeviceIdType.MESH
N = 32
NOPS = 316
LIST = 32
MERGE = 0.35

HOPS = (
    (2, 2),
    (2, 1), (2, 3), (1, 2), (3, 2),
    (0, 2), (2, 0),
    (1, 3), (3, 1),
    (1, 1), (3, 3),
    (0, 1), (0, 3), (1, 0), (3, 0),
)

OFFSETS = tuple((dz, dx, dc) for dz, dx in HOPS for dc in range(2)) + ((0, 0, 1),)


def dot(a, b):
    return lax.dot_general(a, b, (((1,), (0,)), ((), ())), preferred_element_type=F32)


def dot_t(a, b):
    return lax.dot_general(a, b, (((0,), (0,)), ((), ())), preferred_element_type=F32)


def split(x):
    hi = x.astype(BF16)
    lo = (x - hi.astype(F32)).astype(BF16)
    return hi, lo


def split3(x):
    hi = x.astype(BF16)
    rest = x - hi.astype(F32)
    mid = rest.astype(BF16)
    lo = (rest - mid.astype(F32)).astype(BF16)
    return hi, mid, lo


def cos_sin(angle):
    h = angle * 0.5
    g = h * h
    s = 1.0 / 6227020800.0
    for c in (-1.0 / 39916800.0, 1.0 / 362880.0, -1.0 / 5040.0, 1.0 / 120.0, -1.0 / 6.0, 1.0):
        s = s * g + c
    s = s * h
    c0 = 1.0 / 479001600.0
    for c in (-1.0 / 3628800.0, 1.0 / 40320.0, -1.0 / 720.0, 1.0 / 24.0, -0.5, 1.0):
        c0 = c0 * g + c
    return 1.0 - 2.0 * s * s, 2.0 * s * c0


def iota(shape, dim):
    return lax.broadcasted_iota(jnp.int32, shape, dim)


def onehot(cond):
    return jnp.where(cond, 1.0, 0.0).astype(F32).astype(BF16)


def kernel(
    leaves_hbm, theta_a_hbm, phi_a_hbm, shift_b_hbm, theta_b_hbm, phi_b_hbm, shift_c_hbm,
    pmap_hbm, list_hbm, ops_hbm, trans_hbm,
    parents_ref, recv_c,
    leaves, theta_a, phi_a, shift_b, theta_b, phi_b, shift_c, pmap, ilist, iops, trans,
    q3, w3, v3, tab, middle, gains, cs,
    buf_a, held_a, recv_a, buf_b, held_b, recv_b, buf_c, azi, group, total,
    in_sem, leaf_sem, send_held, got_held, send_a, got_a, send_b, got_b, send_c, got_c,
):
    me = lax.axis_index("box")
    z, x, core = me // 8, (me // 2) % 4, me % 2
    zs = [((z + k) % 4) * 8 for k in range(4)]
    xs = [((x + k) % 4) * 2 for k in range(4)]
    cores = [core, 1 - core]

    def device(dz, dx, dc):
        return zs[dz] + xs[dx] + cores[dc]

    partners = [device(*offset) for offset in OFFSETS]
    relays, origins, near, far = [], [], [], []
    for q in range(4):
        axis, step = ((0, 1), (1, 3), (0, 3), (1, 1))[q]
        ahead = [0, 0, 0]
        ahead[axis] = step
        behind = [0, 0, 0]
        behind[axis] = 4 - step
        relays.append(device(*ahead))
        origins.append(device(*behind))
        near.append([device(*offset) for offset in OFFSETS if offset[axis] in (0, 4 - step)])
        far.append([device(*offset) for offset in OFFSETS if offset[axis] in (0, step)])

    def fetch(k, src, dst):
        copy = pltpu.make_async_copy(src, dst, in_sem.at[k])
        copy.start()
        return copy

    def fetch_leaves(q):
        copy = pltpu.make_async_copy(
            leaves_hbm.at[pl.ds(8 * q, 8)], leaves.at[pl.ds(8 * q, 8)], leaf_sem.at[q]
        )
        copy.start()
        return copy

    get_shift_b = fetch(2, shift_b_hbm, shift_b)
    get_phi_a = fetch(1, phi_a_hbm, phi_a)
    get_theta_a = fetch(0, theta_a_hbm, theta_a)
    get_leaves = [fetch_leaves(0)]

    barrier = pltpu.get_barrier_semaphore()
    for d in partners:
        pl.semaphore_signal(barrier, inc=1, device_id={"box": d}, device_id_type=MESH)

    get_theta_b = fetch(3, theta_b_hbm, theta_b)
    get_leaves += [fetch_leaves(q) for q in range(1, 4)]
    get_trans = fetch(4, trans_hbm, trans)
    get_list = fetch(5, list_hbm, ilist)
    get_ops = fetch(6, ops_hbm, iops)
    get_phi_b = fetch(7, phi_b_hbm, phi_b)
    get_pmap = fetch(8, pmap_hbm, pmap)
    get_shift_c = fetch(
        9, shift_c_hbm.at[:, pl.ds(pl.multiple_of(8 * (me // 2), 8), 8), :], shift_c
    )

    get_phi_a.wait()
    for i, half in enumerate(split(phi_a[...])):
        none = jnp.zeros_like(half)
        both = jnp.concatenate(
            [jnp.concatenate([half, none], 1), jnp.concatenate([none, half], 1)], 0
        )
        if i == 0:
            q3[0:128, :] = both
            q3[128:256, :] = both
        else:
            q3[256:384, :] = both

    get_theta_a.wait()
    col = iota((32, 128), 1)
    pick_t = onehot(iota((32, 128), 0) == 2 * ((col % 64) // 4) + col // 64)
    rep_u = onehot(iota((256, 64), 1) == iota((256, 64), 0) // 4)
    same = iota((256, 128), 0) % 4 == iota((256, 128), 1) % 4
    for i, half in enumerate(split(theta_a[...])):
        wide = dot(rep_u, dot_t(half, pick_t).astype(BF16))
        wide = jnp.where(same, wide, 0.0).astype(BF16)
        if i == 0:
            w3[:, 0:128] = wide
            w3[:, 256:384] = wide
        else:
            w3[:, 128:256] = wide

    get_shift_b.wait()
    rep_u3 = jnp.concatenate([rep_u, rep_u, rep_u], 1)

    @pl.loop(0, 8, unroll=True)
    def _(o):
        cosine, sine = cos_sin(shift_b[o])
        pair = MERGE * jnp.concatenate([cosine, sine], 1)
        tab[o] = dot(rep_u3, jnp.concatenate(split3(pair), 0))

    def middle_matrix():
        get_theta_b.wait()
        pick_u = onehot(iota((64, 256), 0) == iota((64, 256), 1) // 4)
        row = iota((512, 128), 0)
        rep_u2 = onehot(iota((512, 128), 1) == 4 * (row // 16) + row % 4)
        same = (iota((512, 256), 0) % 16) // 4 == iota((512, 256), 1) % 4
        for i, half in enumerate(split(theta_b[...])):
            wide = dot(rep_u2, dot_t(half, pick_u).astype(BF16))
            wide = jnp.where(same, wide, 0.0).astype(BF16)
            if i == 0:
                v3[:, 0:256] = wide
                v3[:, 512:768] = wide
            else:
                v3[:, 256:512] = wide

    def merge(q):
        def one_leaf(o):
            pattern = leaves[8 * q + o].reshape(128, 128)
            hi, lo = split(pattern)
            y = dot(jnp.concatenate([hi, lo, hi], 1), q3[...])
            y = jnp.concatenate(
                [
                    jnp.concatenate([y[0:64, 0:128], y[64:128, 0:128]], 1),
                    jnp.concatenate([y[0:64, 128:256], y[64:128, 128:256]], 1),
                ],
                0,
            )
            hi, lo = split(y)
            up = dot(w3[...], jnp.concatenate([hi, hi, lo], 0))
            cosine, sine = tab[o, :, 0:128], tab[o, :, 128:256]
            re, im = up[:, 0:128], up[:, 128:256]
            middle[q, :, 0:128] += cosine * re - sine * im
            middle[q, :, 128:256] += sine * re + cosine * im

        middle[q] = jnp.zeros((256, 256), F32)
        for o in range(8):
            one_leaf(o)
        for c in range(2):
            buf_a[q, :, c] = middle[q, :, 128 * c : 128 * c + 128].reshape(32, 8, 128)
        recv_a[4 * me + q] = buf_a[q, me]

    def raise_polar(q, rows, raised, origin):
        both = [rows[q, :, c].reshape(256, 128) for c in range(2)]
        hi, lo = split(jnp.concatenate(both, 1))
        polar = dot(v3[...], jnp.concatenate([hi, hi, lo], 0))
        for c in range(2):
            raised[q, :, c] = polar[:, 128 * c : 128 * c + 128].reshape(32, 16, 128)
        recv_b[4 * origin + q] = raised[q, me]

    def send(buf, origin, q, targets, recv, send_sem, got_sem):
        for d in targets:
            pltpu.make_async_remote_copy(
                src_ref=buf.at[q, d],
                dst_ref=recv.at[4 * origin + q],
                send_sem=send_sem,
                recv_sem=got_sem,
                device_id={"box": d},
                device_id_type=MESH,
            ).start()

    hand_on = [
        pltpu.make_async_remote_copy(
            src_ref=buf_a.at[q],
            dst_ref=held_a.at[q],
            send_sem=send_held.at[q],
            recv_sem=got_held.at[q],
            device_id={"box": relays[q]},
            device_id_type=MESH,
        )
        for q in range(4)
    ]

    def near_polar(q):
        raise_polar(q, buf_a, buf_b, me)
        send(buf_b, me, q, near[q], recv_b, send_b, got_b.at[q])

    for q in range(4):
        get_leaves[q].wait()
        merge(q)
        if q == 0:
            pl.semaphore_wait(barrier, N - 1)
        hand_on[q].start()
        send(buf_a, me, q, near[q], recv_a, send_a, got_a)
        if q == 0:
            middle_matrix()
            near_polar(0)

    def far_rows(q):
        hand_on[q].wait_recv()
        send(held_a, origins[q], q, far[q], recv_a, send_a, got_a)
        recv_a[4 * origins[q] + q] = held_a[q, me]

    def far_polar(q):
        raise_polar(q, held_a, held_b, origins[q])
        send(held_b, origins[q], q, far[q], recv_b, send_b, got_b.at[q])

    far_rows(0)
    near_polar(1)
    far_rows(1)
    near_polar(2)
    far_rows(2)
    far_polar(0)
    far_rows(3)
    far_polar(1)
    near_polar(3)
    far_polar(2)
    far_polar(3)

    get_trans.wait()
    upper = iota((8, 128), 0) < 4

    @pl.loop(0, NOPS // 4)
    def _(k):
        for j in range(4):
            for c in range(2):
                two = trans[c, 4 * k + j]
                gains[4 * k + j, c] = jnp.where(
                    upper,
                    jnp.broadcast_to(two[0:1], (8, 128)),
                    jnp.broadcast_to(two[1:2], (8, 128)),
                )

    def every(ref, send_sem, got_sem):
        return pltpu.make_async_remote_copy(
            src_ref=ref,
            dst_ref=ref,
            send_sem=send_sem,
            recv_sem=got_sem,
            device_id={"box": partners[-1]},
            device_id_type=MESH,
        )

    all_a = every(recv_a.at[pl.ds(0, 120)], send_a, got_a)
    sent_b = every(buf_b.at[:, pl.ds(0, 30)], send_b, got_b.at[0])
    rounds_b = [every(buf_b.at[0, pl.ds(0, 30)], send_b, got_b.at[q]) for q in range(4)]
    all_c = every(recv_c.at[:, :, pl.ds(0, 248), :], send_c, got_c)
    get_list.wait()
    get_ops.wait()
    all_a.wait_recv()

    def translate(d, put):
        @pl.loop(0, 4)
        def _(k):
            t = 4 * d + k
            sums = [jnp.zeros((8, 128), F32) for _ in range(4)]
            for j in range(LIST):
                s, o = ilist[j, t], iops[j, t]
                sr, si = recv_a[s, 0], recv_a[s, 1]
                gr, gi = gains[o, 0], gains[o, 1]
                sums[0] += gr * sr
                sums[1] += gi * si
                sums[2] += gr * si
                sums[3] += gi * sr
            put(k, sums[0] - sums[1], sums[2] + sums[3])

    for d in partners:

        def put(k, re, im, d=d):
            buf_c[d, k, 0] = re
            buf_c[d, k, 1] = im

        translate(d, put)
        pltpu.make_async_remote_copy(
            src_ref=buf_c.at[d],
            dst_ref=recv_c.at[:, :, pl.ds(pl.multiple_of(8 * me, 8), 8), :],
            send_sem=send_c,
            recv_sem=got_c,
            device_id={"box": d},
            device_id_type=MESH,
        ).start()

    def put_own(k, re, im):
        recv_c[k, 0, pl.ds(pl.multiple_of(8 * me, 8), 8), :] = re
        recv_c[k, 1, pl.ds(pl.multiple_of(8 * me, 8), 8), :] = im

    translate(me, put_own)

    get_phi_b.wait()
    hi, lo = split(phi_b[...])
    azi[0:128, :] = hi
    azi[128:256, :] = hi
    azi[256:384, :] = lo
    get_shift_c.wait()
    upper_half = core == 0
    for o in range(8):
        pair = MERGE * jnp.concatenate(cos_sin(shift_c[o]), 1)
        four = jnp.where(upper_half, pair[0:4], pair[4:8])
        cs[o] = jnp.concatenate([four] * 4, 0)
    get_pmap.wait()
    owner = onehot(iota((16, 128), 0) == pmap[...])
    rep_p = onehot(iota((256, 16), 1) == iota((256, 16), 0) // 16)
    owner_rows = dot(rep_p, owner).astype(BF16)
    same = iota((256, 256), 0) % 16 == iota((256, 256), 1) % 16
    box = iota((128, 256), 0)
    slot = iota((128, 256), 1) // 16
    total[...] = jnp.zeros_like(total)

    def merge_octant(o):
        pick_box = onehot(box == 8 * slot + o)
        pick = jnp.where(same, dot(owner_rows, pick_box), 0.0).astype(BF16)
        rows = [
            jnp.concatenate([recv_b[8 * m + o, 0], recv_b[8 * m + o, 1]], 1) for m in range(16)
        ]
        hi, lo = split(jnp.concatenate(rows, 0))
        merged = dot(jnp.concatenate([pick, pick], 1), jnp.concatenate([hi, lo], 0))
        cosine, sine = cs[o, :, 0:256], cs[o, :, 256:512]
        group[0:256, :] = merged[:, 0:128]
        group[256:512, :] = merged[:, 128:256]
        for h in range(2):
            parts = []
            for c in range(2):
                hi, lo = split(group[256 * c + 128 * h : 256 * c + 128 * h + 128, :])
                parts.append(
                    dot(jnp.concatenate([hi, lo, hi], 1), azi[...]).reshape(8, 16, 256)
                )
            re, im = parts
            for c, turned in enumerate(
                (cosine * re - sine * im, sine * re + cosine * im)
            ):
                total[pl.ds(8 * h, 8), c] += turned

    for q in range(4):
        rounds_b[q].wait_recv()
        merge_octant(q)
        merge_octant(q + 4)

    for i in range(4):
        parents_ref[:, :, i] = total[:, :, 4 * i : 4 * i + 4, :]

    all_c.wait_recv()
    for q in range(4):
        hand_on[q].wait_send()
    all_a.wait_send()
    sent_b.wait_send()
    all_c.wait_send()


def write(parents_in, rows_in, parents_hbm, incoming_hbm, rows, sem):
    copies = [pltpu.make_async_copy(parents_in, parents_hbm, sem.at[4])]
    copies[0].start()
    for k in range(4):
        for c in range(2):
            for i in range(4):
                rows[k, c, i] = rows_in[k, c, pl.ds(i, 64, stride=4), :]
        copies.append(pltpu.make_async_copy(rows.at[k], incoming_hbm.at[k], sem.at[k]))
        copies[-1].start()
    for copy in copies:
        copy.wait()


def on_device(
    leaves, theta_a, phi_a, shift_b, theta_b, phi_b, shift_c, parent_map, inter_list, op_index,
    trans_ops,
):
    grid = leaves.reshape(32, 2, 4, 16, 128).transpose(0, 1, 3, 2, 4).reshape(32, 2, 64, 128)
    hbm = pl.BlockSpec(memory_space=pltpu.HBM)
    vmem = pl.BlockSpec(memory_space=pltpu.VMEM)

    def v(*shape, kind=F32):
        return pltpu.VMEM(shape, kind)

    dma = pltpu.SemaphoreType.DMA
    parents, rows = pl.pallas_call(
        kernel,
        out_shape=(
            pltpu.VMEM((16, 2, 4, 4, 256), F32),
            pltpu.VMEM((4, 2, 256, 128), F32),
        ),
        in_specs=[hbm] * 11,
        out_specs=(vmem, vmem),
        scratch_shapes=[
            v(32, 2, 64, 128), v(32, 64), v(64, 128), v(8, 64, 128), v(64, 128), v(128, 256),
            v(8, 8, 256), v(1, 128, kind=jnp.int32),
            pltpu.SMEM((LIST, 128), jnp.int32), pltpu.SMEM((LIST, 128), jnp.int32),
            v(2, NOPS, 2, 128),
            v(384, 256, kind=BF16), v(256, 384, kind=BF16), v(512, 768, kind=BF16),
            v(8, 256, 256), v(4, 256, 256), v(NOPS, 2, 8, 128), v(8, 16, 512),
            v(4, 32, 2, 8, 128), v(4, 32, 2, 8, 128), v(128, 2, 8, 128),
            v(4, 32, 2, 16, 128), v(4, 32, 2, 16, 128), v(128, 2, 16, 128),
            v(32, 4, 2, 8, 128),
            v(384, 256, kind=BF16), v(512, 128), v(16, 2, 16, 256),
            dma((10,)), dma((4,)), dma((4,)), dma((4,)), dma, dma, dma, dma((4,)), dma, dma,
        ],
        compiler_params=pltpu.CompilerParams(
            collective_id=0, has_side_effects=True, vmem_limit_bytes=56 * 2**20
        ),
    )(
        grid, theta_a, phi_a, shift_b, theta_b, phi_b, shift_c, parent_map.reshape(1, 128),
        inter_list.T, op_index.T, trans_ops,
    )
    return pl.pallas_call(
        write,
        out_shape=(
            jax.ShapeDtypeStruct((16, 2, 4, 4, 256), F32),
            jax.ShapeDtypeStruct((4, 2, 4, 64, 128), F32),
        ),
        in_specs=[vmem, vmem],
        out_specs=(hbm, hbm),
        scratch_shapes=[v(4, 2, 4, 64, 128), dma((5,))],
        compiler_params=pltpu.CompilerParams(vmem_limit_bytes=8 * 2**20),
    )(parents, rows)


def solution(mesh):
    r = P()
    in_specs = (P("box", None, "inc", None),) + (r,) * 9 + (P(None, None, "box", None),)
    out_specs = (P(None, None, "inc", "box", None), P("box", None, "inc", None, None))
    return jax.shard_map(
        on_device, mesh=mesh, in_specs=in_specs, out_specs=out_specs, check_vma=False
    )
```

```python
import functools

import jax
import jax.numpy as jnp
from jax import lax
from jax.experimental import pallas as pl
from jax.experimental.pallas import tpu as pltpu
from jax.sharding import PartitionSpec as P

F32 = jnp.float32
BF16 = jnp.bfloat16
MESH = pl.DeviceIdType.MESH
N = 32
NOPS = 316
LIST = 32
MERGE = 0.35

HOPS = (
    (2, 2),
    (2, 1), (2, 3), (1, 2), (3, 2),
    (0, 2), (2, 0),
    (1, 3), (3, 1),
    (1, 1), (3, 3),
    (0, 1), (0, 3), (1, 0), (3, 0),
)

OFFSETS = tuple((dz, dx, dc) for dz, dx in HOPS for dc in range(2)) + ((0, 0, 1),)


def dot(a, b):
    return lax.dot_general(a, b, (((1,), (0,)), ((), ())), preferred_element_type=F32)


def dot_t(a, b):
    return lax.dot_general(a, b, (((0,), (0,)), ((), ())), preferred_element_type=F32)


def split(x):
    hi = x.astype(BF16)
    lo = (x - hi.astype(F32)).astype(BF16)
    return hi, lo


def split3(x):
    hi = x.astype(BF16)
    rest = x - hi.astype(F32)
    mid = rest.astype(BF16)
    lo = (rest - mid.astype(F32)).astype(BF16)
    return hi, mid, lo


def cos_sin(angle):
    h = angle * 0.5
    g = h * h
    s = 1.0 / 6227020800.0
    for c in (-1.0 / 39916800.0, 1.0 / 362880.0, -1.0 / 5040.0, 1.0 / 120.0, -1.0 / 6.0, 1.0):
        s = s * g + c
    s = s * h
    c0 = 1.0 / 479001600.0
    for c in (-1.0 / 3628800.0, 1.0 / 40320.0, -1.0 / 720.0, 1.0 / 24.0, -0.5, 1.0):
        c0 = c0 * g + c
    return 1.0 - 2.0 * s * s, 2.0 * s * c0


def iota(shape, dim):
    return lax.broadcasted_iota(jnp.int32, shape, dim)


def onehot(cond):
    return jnp.where(cond, 1.0, 0.0).astype(F32).astype(BF16)


def kernel(
    leaves_hbm, theta_a_hbm, phi_a_hbm, shift_b_hbm, theta_b_hbm, phi_b_hbm, shift_c_hbm,
    pmap_hbm, list_hbm, ops_hbm, trans_hbm,
    parents_ref, recv_c,
    leaves, theta_a, phi_a, shift_b, theta_b, phi_b, shift_c, pmap, ilist, iops, trans,
    q3, w3, v3, tab, middle, gains, cs,
    buf_a, held_a, recv_a, buf_b, held_b, recv_b, buf_c, azi, group, total,
    in_sem, leaf_sem, send_held, got_held, send_a, got_a, send_b, got_b, send_c, got_c,
):
    me = lax.axis_index("box")
    z, x, core = me // 8, (me // 2) % 4, me % 2
    sign = 1 - 2 * core
    zs = [((z + 4 + sign * k) % 4) * 8 for k in range(4)]
    xs = [((x + 4 + sign * k) % 4) * 2 for k in range(4)]
    cores = [core, 1 - core]

    def device(dz, dx, dc):
        return zs[dz] + xs[dx] + cores[dc]

    partners = [device(*offset) for offset in OFFSETS]
    relays, origins, near, far = [], [], [], []
    for q in range(4):
        axis, step = ((0, 1), (1, 3), (0, 3), (1, 1))[q]
        ahead = [0, 0, 0]
        ahead[axis] = step
        behind = [0, 0, 0]
        behind[axis] = 4 - step
        relays.append(device(*ahead))
        origins.append(device(*behind))
        near.append([device(*offset) for offset in OFFSETS if offset[axis] in (0, 4 - step)])
        far.append([device(*offset) for offset in OFFSETS if offset[axis] in (0, step)])

    def fetch(k, src, dst):
        copy = pltpu.make_async_copy(src, dst, in_sem.at[k])
        copy.start()
        return copy

    def fetch_leaves(q):
        copy = pltpu.make_async_copy(
            leaves_hbm.at[pl.ds(8 * q, 8)], leaves.at[pl.ds(8 * q, 8)], leaf_sem.at[q]
        )
        copy.start()
        return copy

    get_shift_b = fetch(2, shift_b_hbm, shift_b)
    get_phi_a = fetch(1, phi_a_hbm, phi_a)
    get_theta_a = fetch(0, theta_a_hbm, theta_a)
    get_leaves = [fetch_leaves(0)]

    barrier = pltpu.get_barrier_semaphore()
    for d in partners:
        pl.semaphore_signal(barrier, inc=1, device_id={"box": d}, device_id_type=MESH)

    get_theta_b = fetch(3, theta_b_hbm, theta_b)
    get_leaves += [fetch_leaves(q) for q in range(1, 4)]
    get_trans = fetch(4, trans_hbm, trans)
    get_list = fetch(5, list_hbm, ilist)
    get_ops = fetch(6, ops_hbm, iops)
    get_phi_b = fetch(7, phi_b_hbm, phi_b)
    get_pmap = fetch(8, pmap_hbm, pmap)
    get_shift_c = fetch(
        9, shift_c_hbm.at[:, pl.ds(pl.multiple_of(8 * (me // 2), 8), 8), :], shift_c
    )

    get_phi_a.wait()
    for i, half in enumerate(split(phi_a[...])):
        none = jnp.zeros_like(half)
        both = jnp.concatenate(
            [jnp.concatenate([half, none], 1), jnp.concatenate([none, half], 1)], 0
        )
        if i == 0:
            q3[0:128, :] = both
            q3[128:256, :] = both
        else:
            q3[256:384, :] = both

    get_theta_a.wait()
    col = iota((32, 128), 1)
    pick_t = onehot(iota((32, 128), 0) == 2 * ((col % 64) // 4) + col // 64)
    rep_u = onehot(iota((256, 64), 1) == iota((256, 64), 0) // 4)
    same = iota((256, 128), 0) % 4 == iota((256, 128), 1) % 4
    for i, half in enumerate(split(theta_a[...])):
        wide = dot(rep_u, dot_t(half, pick_t).astype(BF16))
        wide = jnp.where(same, wide, 0.0).astype(BF16)
        if i == 0:
            w3[:, 0:128] = wide
            w3[:, 256:384] = wide
        else:
            w3[:, 128:256] = wide

    get_shift_b.wait()
    rep_u3 = jnp.concatenate([rep_u, rep_u, rep_u], 1)

    @pl.loop(0, 8, unroll=True)
    def _(o):
        cosine, sine = cos_sin(shift_b[o])
        pair = MERGE * jnp.concatenate([cosine, sine], 1)
        tab[o] = dot(rep_u3, jnp.concatenate(split3(pair), 0))

    def middle_matrix():
        get_theta_b.wait()
        pick_u = onehot(iota((64, 256), 0) == iota((64, 256), 1) // 4)
        row = iota((512, 128), 0)
        rep_u2 = onehot(iota((512, 128), 1) == 4 * (row // 16) + row % 4)
        same = (iota((512, 256), 0) % 16) // 4 == iota((512, 256), 1) % 4
        for i, half in enumerate(split(theta_b[...])):
            wide = dot(rep_u2, dot_t(half, pick_u).astype(BF16))
            wide = jnp.where(same, wide, 0.0).astype(BF16)
            if i == 0:
                v3[:, 0:256] = wide
                v3[:, 512:768] = wide
            else:
                v3[:, 256:512] = wide

    def merge(q):
        def one_leaf(o):
            pattern = leaves[8 * q + o].reshape(128, 128)
            hi, lo = split(pattern)
            y = dot(jnp.concatenate([hi, lo, hi], 1), q3[...])
            y = jnp.concatenate(
                [
                    jnp.concatenate([y[0:64, 0:128], y[64:128, 0:128]], 1),
                    jnp.concatenate([y[0:64, 128:256], y[64:128, 128:256]], 1),
                ],
                0,
            )
            hi, lo = split(y)
            up = dot(w3[...], jnp.concatenate([hi, hi, lo], 0))
            cosine, sine = tab[o, :, 0:128], tab[o, :, 128:256]
            re, im = up[:, 0:128], up[:, 128:256]
            middle[q, :, 0:128] += cosine * re - sine * im
            middle[q, :, 128:256] += sine * re + cosine * im

        middle[q] = jnp.zeros((256, 256), F32)
        for o in range(8):
            one_leaf(o)
        for c in range(2):
            buf_a[q, :, c] = middle[q, :, 128 * c : 128 * c + 128].reshape(32, 8, 128)
        recv_a[4 * me + q] = buf_a[q, me]

    def raise_polar(q, rows, raised, origin):
        both = [rows[q, :, c].reshape(256, 128) for c in range(2)]
        hi, lo = split(jnp.concatenate(both, 1))
        polar = dot(v3[...], jnp.concatenate([hi, hi, lo], 0))
        for c in range(2):
            raised[q, :, c] = polar[:, 128 * c : 128 * c + 128].reshape(32, 16, 128)
        recv_b[4 * origin + q] = raised[q, me]

    def send(buf, origin, q, targets, recv, send_sem, got_sem):
        for d in targets:
            pltpu.make_async_remote_copy(
                src_ref=buf.at[q, d],
                dst_ref=recv.at[4 * origin + q],
                send_sem=send_sem,
                recv_sem=got_sem,
                device_id={"box": d},
                device_id_type=MESH,
            ).start()

    hand_on = [
        pltpu.make_async_remote_copy(
            src_ref=buf_a.at[q],
            dst_ref=held_a.at[q],
            send_sem=send_held.at[q],
            recv_sem=got_held.at[q],
            device_id={"box": relays[q]},
            device_id_type=MESH,
        )
        for q in range(4)
    ]

    def near_polar(q):
        raise_polar(q, buf_a, buf_b, me)
        send(buf_b, me, q, near[q], recv_b, send_b, got_b.at[q])

    for q in range(4):
        get_leaves[q].wait()
        merge(q)
        if q == 0:
            pl.semaphore_wait(barrier, N - 1)
        hand_on[q].start()
        send(buf_a, me, q, near[q], recv_a, send_a, got_a)
        if q == 0:
            middle_matrix()
            near_polar(0)

    def far_rows(q):
        hand_on[q].wait_recv()
        send(held_a, origins[q], q, far[q], recv_a, send_a, got_a)
        recv_a[4 * origins[q] + q] = held_a[q, me]

    def far_polar(q):
        raise_polar(q, held_a, held_b, origins[q])
        send(held_b, origins[q], q, far[q], recv_b, send_b, got_b.at[q])

    far_rows(0)
    near_polar(1)
    far_rows(1)
    near_polar(2)
    far_rows(2)
    far_polar(0)
    far_rows(3)
    far_polar(1)
    near_polar(3)
    far_polar(2)
    far_polar(3)

    get_trans.wait()
    upper = iota((8, 128), 0) < 4

    @pl.loop(0, NOPS // 4)
    def _(k):
        for j in range(4):
            for c in range(2):
                two = trans[c, 4 * k + j]
                gains[4 * k + j, c] = jnp.where(
                    upper,
                    jnp.broadcast_to(two[0:1], (8, 128)),
                    jnp.broadcast_to(two[1:2], (8, 128)),
                )

    def every(ref, send_sem, got_sem):
        return pltpu.make_async_remote_copy(
            src_ref=ref,
            dst_ref=ref,
            send_sem=send_sem,
            recv_sem=got_sem,
            device_id={"box": partners[-1]},
            device_id_type=MESH,
        )

    all_a = every(recv_a.at[pl.ds(0, 120)], send_a, got_a)
    sent_b = every(buf_b.at[:, pl.ds(0, 30)], send_b, got_b.at[0])
    rounds_b = [every(buf_b.at[0, pl.ds(0, 30)], send_b, got_b.at[q]) for q in range(4)]
    all_c = every(recv_c.at[:, :, pl.ds(0, 248), :], send_c, got_c)
    get_list.wait()
    get_ops.wait()
    all_a.wait_recv()

    def translate(d, put):
        @pl.loop(0, 4)
        def _(k):
            t = 4 * d + k
            sums = [jnp.zeros((8, 128), F32) for _ in range(4)]
            for j in range(LIST):
                s, o = ilist[j, t], iops[j, t]
                sr, si = recv_a[s, 0], recv_a[s, 1]
                gr, gi = gains[o, 0], gains[o, 1]
                sums[0] += gr * sr
                sums[1] += gi * si
                sums[2] += gr * si
                sums[3] += gi * sr
            put(k, sums[0] - sums[1], sums[2] + sums[3])

    for d in partners:

        def put(k, re, im, d=d):
            buf_c[d, k, 0] = re
            buf_c[d, k, 1] = im

        translate(d, put)
        pltpu.make_async_remote_copy(
            src_ref=buf_c.at[d],
            dst_ref=recv_c.at[:, :, pl.ds(pl.multiple_of(8 * me, 8), 8), :],
            send_sem=send_c,
            recv_sem=got_c,
            device_id={"box": d},
            device_id_type=MESH,
        ).start()

    def put_own(k, re, im):
        recv_c[k, 0, pl.ds(pl.multiple_of(8 * me, 8), 8), :] = re
        recv_c[k, 1, pl.ds(pl.multiple_of(8 * me, 8), 8), :] = im

    translate(me, put_own)

    get_phi_b.wait()
    hi, lo = split(phi_b[...])
    azi[0:128, :] = hi
    azi[128:256, :] = hi
    azi[256:384, :] = lo
    get_shift_c.wait()
    upper_half = core == 0
    for o in range(8):
        pair = MERGE * jnp.concatenate(cos_sin(shift_c[o]), 1)
        four = jnp.where(upper_half, pair[0:4], pair[4:8])
        cs[o] = jnp.concatenate([four] * 4, 0)
    get_pmap.wait()
    owner = onehot(iota((16, 128), 0) == pmap[...])
    rep_p = onehot(iota((256, 16), 1) == iota((256, 16), 0) // 16)
    owner_rows = dot(rep_p, owner).astype(BF16)
    same = iota((256, 256), 0) % 16 == iota((256, 256), 1) % 16
    box = iota((128, 256), 0)
    slot = iota((128, 256), 1) // 16
    total[...] = jnp.zeros_like(total)

    def merge_octant(o):
        pick_box = onehot(box == 8 * slot + o)
        pick = jnp.where(same, dot(owner_rows, pick_box), 0.0).astype(BF16)
        rows = [
            jnp.concatenate([recv_b[8 * m + o, 0], recv_b[8 * m + o, 1]], 1) for m in range(16)
        ]
        hi, lo = split(jnp.concatenate(rows, 0))
        merged = dot(jnp.concatenate([pick, pick], 1), jnp.concatenate([hi, lo], 0))
        cosine, sine = cs[o, :, 0:256], cs[o, :, 256:512]
        group[0:256, :] = merged[:, 0:128]
        group[256:512, :] = merged[:, 128:256]
        for h in range(2):
            parts = []
            for c in range(2):
                hi, lo = split(group[256 * c + 128 * h : 256 * c + 128 * h + 128, :])
                parts.append(
                    dot(jnp.concatenate([hi, lo, hi], 1), azi[...]).reshape(8, 16, 256)
                )
            re, im = parts
            for c, turned in enumerate(
                (cosine * re - sine * im, sine * re + cosine * im)
            ):
                total[pl.ds(8 * h, 8), c] += turned

    for q in range(4):
        rounds_b[q].wait_recv()
        merge_octant(q)
        merge_octant(q + 4)

    for i in range(4):
        parents_ref[:, :, i] = total[:, :, 4 * i : 4 * i + 4, :]

    all_c.wait_recv()
    for q in range(4):
        hand_on[q].wait_send()
    all_a.wait_send()
    sent_b.wait_send()
    all_c.wait_send()


def write(parents_in, rows_in, parents_hbm, incoming_hbm, rows, sem):
    copies = [pltpu.make_async_copy(parents_in, parents_hbm, sem.at[4])]
    copies[0].start()
    for k in range(4):
        for c in range(2):
            for i in range(4):
                rows[k, c, i] = rows_in[k, c, pl.ds(i, 64, stride=4), :]
        copies.append(pltpu.make_async_copy(rows.at[k], incoming_hbm.at[k], sem.at[k]))
        copies[-1].start()
    for copy in copies:
        copy.wait()


def on_device(
    leaves, theta_a, phi_a, shift_b, theta_b, phi_b, shift_c, parent_map, inter_list, op_index,
    trans_ops,
):
    grid = leaves.reshape(32, 2, 4, 16, 128).transpose(0, 1, 3, 2, 4).reshape(32, 2, 64, 128)
    hbm = pl.BlockSpec(memory_space=pltpu.HBM)
    vmem = pl.BlockSpec(memory_space=pltpu.VMEM)

    def v(*shape, kind=F32):
        return pltpu.VMEM(shape, kind)

    dma = pltpu.SemaphoreType.DMA
    parents, rows = pl.pallas_call(
        kernel,
        out_shape=(
            pltpu.VMEM((16, 2, 4, 4, 256), F32),
            pltpu.VMEM((4, 2, 256, 128), F32),
        ),
        in_specs=[hbm] * 11,
        out_specs=(vmem, vmem),
        scratch_shapes=[
            v(32, 2, 64, 128), v(32, 64), v(64, 128), v(8, 64, 128), v(64, 128), v(128, 256),
            v(8, 8, 256), v(1, 128, kind=jnp.int32),
            pltpu.SMEM((LIST, 128), jnp.int32), pltpu.SMEM((LIST, 128), jnp.int32),
            v(2, NOPS, 2, 128),
            v(384, 256, kind=BF16), v(256, 384, kind=BF16), v(512, 768, kind=BF16),
            v(8, 256, 256), v(4, 256, 256), v(NOPS, 2, 8, 128), v(8, 16, 512),
            v(4, 32, 2, 8, 128), v(4, 32, 2, 8, 128), v(128, 2, 8, 128),
            v(4, 32, 2, 16, 128), v(4, 32, 2, 16, 128), v(128, 2, 16, 128),
            v(32, 4, 2, 8, 128),
            v(384, 256, kind=BF16), v(512, 128), v(16, 2, 16, 256),
            dma((10,)), dma((4,)), dma((4,)), dma((4,)), dma, dma, dma, dma((4,)), dma, dma,
        ],
        compiler_params=pltpu.CompilerParams(
            collective_id=0, has_side_effects=True, vmem_limit_bytes=56 * 2**20
        ),
    )(
        grid, theta_a, phi_a, shift_b, theta_b, phi_b, shift_c, parent_map.reshape(1, 128),
        inter_list.T, op_index.T, trans_ops,
    )
    return pl.pallas_call(
        write,
        out_shape=(
            jax.ShapeDtypeStruct((16, 2, 4, 4, 256), F32),
            jax.ShapeDtypeStruct((4, 2, 4, 64, 128), F32),
        ),
        in_specs=[vmem, vmem],
        out_specs=(hbm, hbm),
        scratch_shapes=[v(4, 2, 4, 64, 128), dma((5,))],
        compiler_params=pltpu.CompilerParams(vmem_limit_bytes=8 * 2**20),
    )(parents, rows)


def solution(mesh):
    r = P()
    in_specs = (P("box", None, "inc", None),) + (r,) * 9 + (P(None, None, "box", None),)
    out_specs = (P(None, None, "inc", "box", None), P("box", None, "inc", None, None))
    return jax.shard_map(
        on_device, mesh=mesh, in_specs=in_specs, out_specs=out_specs, check_vma=False
    )
```
